32 devices in a mesh: dp: 1, blk: 16 (over z, x, core), head: 2 (over y).
Axes of the slice: x: 2, y: 2, z: 4, core: 2. Of those that a mesh axis runs over, the one named last changes fastest.
Arguments:
- stored_query_rows: bfloat16 [4096, 8192], P(('dp', 'blk', 'head'))
- stored_key_rows: bfloat16 [4096, 1024], P(('dp', 'blk', 'head'))
- stored_value_rows: bfloat16 [4096, 1024], P(('dp', 'blk', 'head')), may hold values from -6 to 6
- block_docs: int32 [32], P('dp'), may hold values from 0 to 15, never falling along the last dimension, each value on 1 to 4 neighbouring positions
Outputs:
- context: bfloat16 [4096, 8192], P(('dp', 'blk', 'head'))
The draws below stay inside these ranges and needn't reach their ends.
Inputs may be any that keep to these rules, and one draw needn't show every extreme that they name: `block_docs`: document numbers never fall along the sequence; each document covers 1 to 4 blocks, and one covers exactly 4.
All inputs are finite; a program needn't handle non-finite values.
Results may differ from the reference program's by a relative error of at most 0.0045.
Values may be sent and summed in bfloat16 or wider, within the bound.
No kernel may reach another device: no remote copies, remote signals or barrier semaphores. Data moves between devices by JAX's collectives and lax.ppermute only.
A program may use at most 128 MiB of HBM per device.

```python
import math
import jax
import jax.numpy as jnp
import numpy as np
from jax import lax

QUERY_HEADS = 64
KEY_VALUE_HEADS = 8
HEAD_DIMENSION = 128
MASK_BLOCK_SIZE = 128
TOK_DEV = 128
PACKED_TOKENS = 4096
NBLOCKS = 32
DOC_BLOCKS = 4
DOCS = 16
N_BLK = 16


def shared_keys(key):
    block_section = jax.random.fold_in(key, 11)
    block_offset = jax.random.normal(block_section, (PACKED_TOKENS, KEY_VALUE_HEADS * HEAD_DIMENSION), jnp.float32)
    return block_offset


def draw_stored_key_rows(key, part):
    block_offset = shared_keys(key)
    return block_offset.astype(jnp.bfloat16)


def draw_stored_query_rows(key, part):
    block_section = jax.random.fold_in(key, 13)
    drawn = jax.random.normal(block_section, (PACKED_TOKENS, QUERY_HEADS * HEAD_DIMENSION), jnp.float32)
    return drawn.astype(jnp.bfloat16)


def levels(rng, dims, split, least, largest):
    gain, own = 1.0, jax.random.fold_in(rng, 6)
    for dim, parts in split:
        steps = jnp.exp(jax.random.uniform(jax.random.fold_in(own, dim), (parts,), jnp.float32, least / len(split), largest / len(split)))
        gain = gain * jnp.repeat(steps, dims[dim] // parts).reshape([-1 if axis == dim else 1 for axis in range(len(dims))])
    return gain


def split_up(count, total, most, slope):
    weights = [(1 << 20) // math.isqrt(grade ** slope) + 1 for grade in range(2, count + 1)]
    rest, given = total - most - (count - 1), [1] * (count - 1)
    while rest > 0:
        candidates = [i for i in range(count - 1) if given[i] < most]
        pool, remaining = sum([weights[i] for i in candidates]), rest
        for i in candidates:
            more = min(most - given[i], max(1, remaining * weights[i] // pool), rest)
            given[i] = given[i] + more
            rest = rest - more
    return np.array([most] + given)


def uneven_parts(own_key, count, total, bound, slope):
    if count == 2:
        one = jax.random.randint(own_key, (), max(1, total - bound), min(bound, total - 1) + 1)
        return jnp.stack([one, total - one])
    lengths = jnp.asarray(split_up(count, total, bound, slope), jnp.int32)
    twos = (count - 1) // 2
    giver, receiver = lengths[1:1 + 2 * twos:2], lengths[2:2 + 2 * twos:2]
    slack = jnp.minimum(giver - 1, bound - receiver)
    shifted = jax.random.randint(jax.random.fold_in(own_key, 1), (twos,), 0, 1 << 20) % (slack + 1)
    lengths = lengths.at[1:1 + 2 * twos:2].set(giver - shifted).at[2:2 + 2 * twos:2].set(receiver + shifted)
    return lengths[jax.random.permutation(jax.random.fold_in(own_key, 2), count)]


def bell_draw(rng, extent, spread, reach, cuts=(), kind=jnp.bfloat16):
    entries = jax.random.normal(rng, extent, jnp.float32) * spread
    if len(cuts) > 0:
        entries = levels(rng, extent, cuts, -0.22, 0.18) * entries
    return jnp.clip(entries, min=-reach, max=reach).astype(kind)


def setup_inputs(seed: int = 0, part: int = 0) -> dict:
    arg_keys = jax.random.split(jax.random.key(seed), 5)
    own_keys = jax.random.split(jax.random.fold_in(arg_keys[4], part), 5)
    return {
        "stored_query_rows": draw_stored_query_rows(jax.random.fold_in(jax.random.fold_in(arg_keys[4], part), 71), part),
        "stored_key_rows": draw_stored_key_rows(jax.random.fold_in(jax.random.fold_in(arg_keys[4], part), 71), part),
        "stored_value_rows": bell_draw(own_keys[2], (PACKED_TOKENS, KEY_VALUE_HEADS * HEAD_DIMENSION), 1.0, 6.0, ((0, 32),)),
        "block_docs": jnp.searchsorted(jnp.cumsum(uneven_parts(own_keys[3], DOCS, NBLOCKS, DOC_BLOCKS, 2)), jnp.arange(NBLOCKS), side="right").astype(jnp.int32),
    }


def reference(stored_query_rows, stored_key_rows, stored_value_rows, block_docs):
    query_group = QUERY_HEADS // KEY_VALUE_HEADS
    stored = jnp.arange(PACKED_TOKENS, dtype=jnp.int32)
    holder = stored // (2 * TOK_DEV)
    second = stored // TOK_DEV % 2
    piece_index = jnp.where(second == 0, holder, 2 * N_BLK - 1 - holder)
    position = (piece_index * TOK_DEV + stored % TOK_DEV).astype(jnp.int32)
    docs = block_docs[position // MASK_BLOCK_SIZE]
    expanded_keys = stored_key_rows.astype(jnp.float32).reshape(PACKED_TOKENS, KEY_VALUE_HEADS, HEAD_DIMENSION)
    expanded_values = stored_value_rows.astype(jnp.float32).reshape(PACKED_TOKENS, KEY_VALUE_HEADS, HEAD_DIMENSION)
    scale = 1.0 / math.sqrt(HEAD_DIMENSION)

    def one_block(index):
        first_token = (index * MASK_BLOCK_SIZE).astype(jnp.int32)
        query_block_rows = lax.dynamic_slice_in_dim(stored_query_rows, first_token, MASK_BLOCK_SIZE, 0).astype(jnp.float32).reshape(MASK_BLOCK_SIZE, KEY_VALUE_HEADS, query_group, HEAD_DIMENSION)
        query_pos = lax.dynamic_slice_in_dim(position, first_token, MASK_BLOCK_SIZE, 0)
        query_doc = lax.dynamic_slice_in_dim(docs, first_token, MASK_BLOCK_SIZE, 0)
        score = jnp.einsum('qhgd,khd->hgqk', query_block_rows, expanded_keys) * scale
        allowed = (docs[None, :] == query_doc[:, None]) & (position[None, :] <= query_pos[:, None])
        score = jnp.where(allowed, score, -1e+30)
        top = lax.optimization_barrier(jnp.max(score, axis=-1, keepdims=True))
        weight = jnp.where(allowed, jnp.exp(score - top), 0.0)
        total = lax.optimization_barrier(jnp.sum(weight, axis=-1))
        weight_low = lax.optimization_barrier(weight.astype(jnp.bfloat16)).astype(jnp.float32)
        summed = jnp.einsum('hgqk,khd->qhgd', weight_low, expanded_values)
        result = summed / jnp.moveaxis(total, 2, 0)[..., None]
        return result.reshape(MASK_BLOCK_SIZE, QUERY_HEADS * HEAD_DIMENSION).astype(jnp.bfloat16)
    blocks_out = lax.map(one_block, jnp.arange(PACKED_TOKENS // MASK_BLOCK_SIZE, dtype=jnp.int32))
    return blocks_out.reshape(PACKED_TOKENS, QUERY_HEADS * HEAD_DIMENSION)
```

```python
import functools
import math

import jax
import jax.numpy as jnp
from jax import lax
from jax.experimental import pallas as pl
from jax.experimental.pallas import tpu as pltpu
from jax.sharding import PartitionSpec as P

HEAD_DIMENSION = 128
AXES = ("blk", "head")
EXP2_SCALE = math.log2(math.e) / math.sqrt(HEAD_DIMENSION)
VMEM_BYTES = 48 * 2**20


def device_of(piece, blk_count):
    return 2 * piece if piece < blk_count else 2 * (2 * blk_count - 1 - piece) + 1


def as_devices(pairs, blk_count):
    pieces = 2 * blk_count
    kept = [(a, b) for a, b in pairs if 0 <= b < pieces]
    fed = {b for _, b in kept}
    kept += [(pieces - 1 - b, b) for b in range(pieces) if b not in fed]
    return [(device_of(a, blk_count), device_of(b, blk_count)) for a, b in kept]


def my_piece(blk_count):
    index = lax.axis_index("blk")
    return jnp.where(lax.axis_index("head") == 0, index, 2 * blk_count - 1 - index)


def wanted(docs_ref, blk_count, reach):
    piece = my_piece(blk_count)
    doc = docs_ref[piece]
    count = jnp.int32(1)
    for back in range(1, reach):
        same = (piece >= back) & (docs_ref[jnp.maximum(piece - back, 0)] == doc)
        count = count + same.astype(jnp.int32)
    odd = piece % 2
    slots = [count > jnp.where(odd == 1, 1, reach - 1)]
    for step in range(1, reach // 2):
        slots.append(count > 2 * step)
        slots.append(count > 2 * step - 1 + 2 * odd)
    return count, slots


def weigh_kernel(blk_count, reach, group, docs_ref, query_ref, *refs):
    keys, weight_ref = refs[:-1], refs[-1]
    rows = query_ref.shape[0]
    kv_heads = keys[0].shape[1] // HEAD_DIMENSION
    count, slots = wanted(docs_ref, blk_count, reach)
    below = lax.broadcasted_iota(jnp.int32, (rows, rows), 0) >= lax.broadcasted_iota(jnp.int32, (rows, rows), 1)
    width = reach * rows

    def weigh(masked):
        for kv_head in range(kv_heads):
            lanes = pl.ds(kv_head * HEAD_DIMENSION, HEAD_DIMENSION)
            key = jnp.concatenate([ref[:, lanes] for ref in keys], axis=0)
            for head in range(kv_head * group, (kv_head + 1) * group):
                query = query_ref[:, pl.ds(head * HEAD_DIMENSION, HEAD_DIMENSION)]
                score = lax.dot_general(query, key, (((1,), (1,)), ((), ())), preferred_element_type=jnp.float32)
                parts = [jnp.where(below, score[:, :rows], -jnp.inf)]
                for slot in range(1, reach):
                    part = score[:, slot * rows : (slot + 1) * rows]
                    parts.append(jnp.where(slots[slot - 1], part, -jnp.inf) if masked else part)
                score = jnp.concatenate(parts, axis=1)
                top = jnp.max(score, axis=1, keepdims=True)
                weight = jnp.exp2((score - top) * EXP2_SCALE)
                weight_ref[:, pl.ds(head * width, width)] = weight.astype(jnp.bfloat16)

    @pl.when(count == reach)
    def _():
        weigh(False)

    @pl.when(count < reach)
    def _():
        weigh(True)


def sum_kernel(reach, group, weight_ref, *refs):
    values, out_ref = refs[:-1], refs[-1]
    rows = out_ref.shape[0]
    kv_heads = values[0].shape[1] // HEAD_DIMENSION
    width = reach * rows
    ones = jnp.ones((width, HEAD_DIMENSION), jnp.bfloat16)
    for kv_head in range(kv_heads):
        lanes = pl.ds(kv_head * HEAD_DIMENSION, HEAD_DIMENSION)
        value = jnp.concatenate([ref[:, lanes] for ref in values], axis=0)
        value = jnp.concatenate([value, ones], axis=1)
        for head in range(kv_head * group, (kv_head + 1) * group):
            weight = weight_ref[:, pl.ds(head * width, width)]
            both = jnp.dot(weight, value, preferred_element_type=jnp.float32)
            result = both[:, :HEAD_DIMENSION] / both[:, HEAD_DIMENSION:]
            out_ref[:, pl.ds(head * HEAD_DIMENSION, HEAD_DIMENSION)] = result.astype(jnp.bfloat16)


def on_device(blk_count, query, key, value, docs):
    rows, query_width = query.shape
    kv_heads = key.shape[1] // HEAD_DIMENSION
    group = query_width // key.shape[1]
    reach = blk_count // 4
    pieces = range(2 * blk_count)
    kv_step = min(4, kv_heads)
    steps = kv_heads // kv_step

    far = as_devices([(p, p + 1 if p % 2 == 0 else p + reach - 1) for p in pieces], blk_count)
    pair = as_devices([(p, p ^ 1) for p in pieces], blk_count)
    direct = [as_devices([(p, p + 2 * step) for p in pieces], blk_count) for step in range(1, reach // 2)]

    def gather(x):
        near = [lax.ppermute(x, AXES, to) for to in direct]
        return x, near, lax.ppermute(x, AXES, far)

    def complete(own, near, last):
        slots = [own, last]
        for array in near:
            slots += [array, lax.ppermute(array, AXES, pair)]
        return slots

    keys = complete(*gather(key))
    values = complete(*gather(value))
    width = reach * rows

    def across(columns):
        return pl.BlockSpec((rows, columns // steps), lambda step: (0, step))

    weights = pl.pallas_call(
        functools.partial(weigh_kernel, blk_count, reach, group),
        out_shape=jax.ShapeDtypeStruct((rows, kv_heads * group * width), jnp.bfloat16),
        grid=(steps,),
        in_specs=[pl.BlockSpec(memory_space=pltpu.SMEM), across(query_width)] + [across(key.shape[1])] * reach,
        out_specs=across(kv_heads * group * width),
        compiler_params=pltpu.CompilerParams(vmem_limit_bytes=VMEM_BYTES),
        cost_estimate=pl.CostEstimate(
            flops=2 * rows * width * query_width,
            bytes_accessed=2 * rows * (query_width + kv_heads * group * width),
            transcendentals=rows * width * kv_heads * group,
        ),
    )(docs, query, *keys)
    return pl.pallas_call(
        functools.partial(sum_kernel, reach, group),
        out_shape=jax.ShapeDtypeStruct(query.shape, query.dtype),
        grid=(steps,),
        in_specs=[across(kv_heads * group * width)] + [across(value.shape[1])] * reach,
        out_specs=across(query_width),
        compiler_params=pltpu.CompilerParams(vmem_limit_bytes=VMEM_BYTES),
        cost_estimate=pl.CostEstimate(
            flops=2 * rows * width * query_width,
            bytes_accessed=2 * rows * (query_width + kv_heads * group * width),
            transcendentals=0,
        ),
    )(weights, *values)


def solution(mesh):
    placed = P(("dp", "blk", "head"), None)
    return jax.shard_map(
        functools.partial(on_device, mesh.shape["blk"]),
        mesh=mesh,
        in_specs=(placed, placed, placed, P("dp")),
        out_specs=placed,
        check_vma=False,
    )
```

```python
import functools
import math

import jax
import jax.numpy as jnp
import numpy as np
from jax import lax
from jax.experimental import pallas as pl
from jax.experimental.pallas import tpu as pltpu
from jax.sharding import PartitionSpec as P

HEAD_DIMENSION = 128
AXES = ("blk", "head")
EXP2_SCALE = math.log2(math.e) / math.sqrt(HEAD_DIMENSION)
VMEM_BYTES = 24 * 2**20
IN_VMEM = pl.BlockSpec(memory_space=pltpu.VMEM)
ANYWHERE = pl.BlockSpec(memory_space=pl.ANY)
LONG = pl.CostEstimate(flops=10**11, bytes_accessed=10**11, transcendentals=0)


def device_of(piece, blk_count):
    return 2 * piece if piece < blk_count else 2 * (2 * blk_count - 1 - piece) + 1


def as_devices(target_of, blk_count):
    return [(device_of(a, blk_count), device_of(b, blk_count)) for a, b in enumerate(target_of)]


def up_by(step, blk_count):
    pieces = 2 * blk_count
    return [p + step if p + step < pieces else pieces - 1 - p for p in range(pieces)]


def is_late(piece, distance, blk_count):
    turns = (piece < blk_count) & (piece + distance >= blk_count)
    return (piece % 2 == 1) & (piece + distance < 2 * blk_count) & ((piece % 4 == 3) | turns)


def early(distance, blk_count):
    target_of = []
    for p in range(2 * blk_count):
        first = p // blk_count * blk_count
        if p % 2 == 0:
            target_of.append(p + 1)
        elif p % 4 == 3:
            target_of.append(p - 1)
        else:
            target_of.append(first + (p - first + distance) % blk_count)
    return target_of


def late(distance, blk_count):
    above = up_by(distance, blk_count)
    return [p + 1 if p % 2 == 0 else above[p] for p in range(2 * blk_count)]


def my_piece(blk_count):
    index = lax.axis_index("blk")
    return jnp.where(lax.axis_index("head") == 0, index, 2 * blk_count - 1 - index)


def stage_kernel(blk_count, reach, docs_ref, flags_ref, any_late_ref):
    distance = reach - 1
    any_late = jnp.int32(0)
    for p in range(2 * blk_count - distance):
        if is_late(p, distance, blk_count):
            any_late = any_late | (docs_ref[p] == docs_ref[p + distance]).astype(jnp.int32)
    any_late_ref[0] = any_late
    piece = my_piece(blk_count)
    doc = docs_ref[piece]
    count = jnp.int32(1)
    for back in range(1, reach):
        same = (piece >= back) & (docs_ref[jnp.maximum(piece - back, 0)] == doc)
        count = count + same.astype(jnp.int32)
    every = count == reach
    odd = piece % 2
    slots = [count > jnp.where(odd == 1, 1, reach - 1)]
    for step in range(1, reach // 2):
        slots.append(count > 2 * step)
        slots.append(count > 2 * step - 1 + 2 * odd)
    farthest = jnp.maximum(piece - (reach - 1), 0)
    comes_late = every & (odd == 0) & is_late(farthest, reach - 1, blk_count)
    for row, flag in enumerate([every, *slots, comes_late]):
        flags_ref[row] = jnp.full(flags_ref.shape[1:], flag.astype(jnp.int32))


def blank_kernel(*refs):
    pass


def blank(arrays):
    return pl.pallas_call(
        blank_kernel,
        out_shape=tuple(jax.ShapeDtypeStruct(x.shape, x.dtype) for x in arrays),
        out_specs=(ANYWHERE,) * len(arrays),
        name="blank",
    )()


def pull_kernel(*refs):
    count = len(refs) // 2
    copies = [pltpu.make_async_copy(refs[i], refs[count + i], refs[-1].at[i]) for i in range(count)]
    for copy in copies:
        copy.start()
    for copy in copies:
        copy.wait()


def pull(arrays, cost=None):
    return pl.pallas_call(
        pull_kernel,
        out_shape=tuple(pltpu.VMEM(x.shape, x.dtype) for x in arrays),
        in_specs=[ANYWHERE] * len(arrays),
        out_specs=[IN_VMEM] * len(arrays),
        scratch_shapes=[pltpu.SemaphoreType.DMA((len(arrays),))],
        compiler_params=pltpu.CompilerParams(vmem_limit_bytes=2**20),
        cost_estimate=cost,
        name="pull",
    )(*in_hbm(arrays))


def choose_last(flags_ref, last_ref, late_hbm, chosen_ref, sem):
    comes_late = jnp.max(flags_ref[flags_ref.shape[0] - 1]) == 1

    @pl.when(comes_late)
    def _():
        copy = pltpu.make_async_copy(late_hbm, chosen_ref, sem)
        copy.start()
        copy.wait()

    @pl.when(jnp.logical_not(comes_late))
    def _():
        chosen_ref[...] = last_ref[...]


def weigh_kernel(reach, group, kv_step, flags_ref, query_ref, late_hbm, own_ref, last_ref, *refs):
    near, weight_ref, token_ref, chosen_ref, sem = refs[:-4], *refs[-4:]
    token_ref[...] = flags_ref[0]
    choose_last(flags_ref, last_ref, late_hbm, chosen_ref, sem)
    keys = [own_ref, chosen_ref, *near]
    rows = query_ref.shape[0]
    kv_heads = own_ref.shape[1] // HEAD_DIMENSION
    causal = lax.broadcasted_iota(jnp.int32, (rows, rows), 0) >= lax.broadcasted_iota(jnp.int32, (rows, rows), 1)
    every = jnp.max(flags_ref[0]) == 1

    def weigh(masked):
        def one_step(step, _):
            for inner in range(kv_step):
                kv_head = step * kv_step + inner
                lanes = pl.ds(pl.multiple_of(kv_head * HEAD_DIMENSION, HEAD_DIMENSION), HEAD_DIMENSION)
                key = jnp.concatenate([ref[:, lanes] for ref in keys], axis=0)
                for member in range(group):
                    head = kv_head * group + member
                    lanes = pl.ds(pl.multiple_of(head * HEAD_DIMENSION, HEAD_DIMENSION), HEAD_DIMENSION)
                    score = lax.dot_general(
                        query_ref[:, lanes], key, (((1,), (1,)), ((), ())), preferred_element_type=jnp.float32
                    )
                    parts = [jnp.where(causal, score[:, :rows], -jnp.inf)]
                    for slot in range(1, reach):
                        part = score[:, slot * rows : (slot + 1) * rows]
                        if masked:
                            part = jnp.where(flags_ref[slot, 0:1, :] == 1, part, -jnp.inf)
                        parts.append(part)
                    score = jnp.concatenate(parts, axis=1)
                    top = jnp.max(score, axis=1, keepdims=True)
                    weight = jnp.exp2((score - top) * EXP2_SCALE)
                    weight_ref[head] = weight.astype(jnp.bfloat16)
            return 0

        lax.fori_loop(0, kv_heads // kv_step, one_step, 0)

    @pl.when(every)
    def _():
        weigh(False)

    @pl.when(jnp.logical_not(every))
    def _():
        weigh(True)


def sum_kernel(reach, group, kv_step, flags_ref, weight_ref, late_hbm, own_ref, last_ref, *refs):
    near, out_hbm, chosen_ref, out_ref, sem, sems = refs[:-5], *refs[-5:]
    choose_last(flags_ref, last_ref, late_hbm, chosen_ref, sem)
    values = [own_ref, chosen_ref, *near]
    rows = out_ref.shape[0]
    kv_heads = own_ref.shape[1] // HEAD_DIMENSION
    ones = jnp.ones((reach * rows, HEAD_DIMENSION), jnp.bfloat16)
    width = group * HEAD_DIMENSION

    def send(kv_head):
        lanes = pl.ds(pl.multiple_of(kv_head * width, width), width)
        return pltpu.make_async_copy(out_ref.at[:, lanes], out_hbm.at[:, lanes], sems.at[kv_head])

    def one_step(step, _):
        for inner in range(kv_step):
            kv_head = step * kv_step + inner
            lanes = pl.ds(pl.multiple_of(kv_head * HEAD_DIMENSION, HEAD_DIMENSION), HEAD_DIMENSION)
            value = jnp.concatenate([ref[:, lanes] for ref in values], axis=0)
            value = jnp.concatenate([value, ones], axis=1)
            for member in range(group):
                head = kv_head * group + member
                both = jnp.dot(weight_ref[head], value, preferred_element_type=jnp.float32)
                result = both[:, :HEAD_DIMENSION] / both[:, HEAD_DIMENSION:]
                lanes = pl.ds(pl.multiple_of(head * HEAD_DIMENSION, HEAD_DIMENSION), HEAD_DIMENSION)
                out_ref[:, lanes] = result.astype(jnp.bfloat16)
            send(kv_head).start()
        return 0

    lax.fori_loop(0, kv_heads // kv_step, one_step, 0)
    for kv_head in range(kv_heads):
        send(kv_head).wait()


def after_kernel(*refs):
    pass


def after(token, arrays):
    return pl.pallas_call(
        after_kernel,
        out_shape=[jax.ShapeDtypeStruct(x.shape, x.dtype) for x in arrays],
        in_specs=[ANYWHERE] * (1 + len(arrays)),
        out_specs=[ANYWHERE] * len(arrays),
        input_output_aliases={1 + index: index for index in range(len(arrays))},
        compiler_params=pltpu.CompilerParams(vmem_limit_bytes=2**20),
        name="after",
    )(*in_vmem([token]), *arrays)


def in_vmem(arrays):
    return [pltpu.with_memory_space_constraint(x, pltpu.VMEM) for x in arrays]


def in_hbm(arrays):
    return [pltpu.with_memory_space_constraint(x, pltpu.HBM) for x in arrays]


def on_device(blk_count, query, key, value, docs):
    rows, query_width = query.shape
    kv_heads = key.shape[1] // HEAD_DIMENSION
    group = query_width // key.shape[1]
    heads = kv_heads * group
    reach = blk_count // 4
    distance = reach - 1
    kv_step = min(4, kv_heads)
    bf16 = jnp.bfloat16

    def sent(x, target_of):
        return lax.ppermute(x, AXES, as_devices(target_of, blk_count))

    pair = [p ^ 1 for p in range(2 * blk_count)]

    def fetch(x):
        near = [sent(x, up_by(2 * step, blk_count)) for step in range(1, reach // 2)]
        return near, sent(x, early(distance, blk_count))

    def with_pairs(near):
        return [x for array in near for x in (array, sent(array, pair))]

    key_near, key_last = fetch(key)
    value_near, value_last = fetch(value)

    flags, any_late = pl.pallas_call(
        functools.partial(stage_kernel, blk_count, reach),
        out_shape=(pltpu.VMEM((reach + 1, 8, rows), jnp.int32), jax.ShapeDtypeStruct((1,), jnp.int32)),
        in_specs=[pl.BlockSpec(memory_space=pltpu.SMEM)],
        out_specs=[IN_VMEM, pl.BlockSpec(memory_space=pltpu.SMEM)],
        compiler_params=pltpu.CompilerParams(vmem_limit_bytes=2**20),
        name="stage",
    )(docs)
    any_late = any_late[0] > 0
    if lax.axis_size("dp") > 1:
        any_late = lax.pmax(any_late.astype(jnp.float32), "dp") > 0
    key_late, value_late = lax.cond(
        any_late,
        lambda: (sent(key, late(distance, blk_count)), sent(value, late(distance, blk_count))),
        lambda: blank((key, value)),
    )

    query, key = pull((query, key), LONG)
    weights, token = pl.pallas_call(
        functools.partial(weigh_kernel, reach, group, kv_step),
        out_shape=(pltpu.VMEM((heads, rows, reach * rows), bf16), pltpu.VMEM((8, rows), jnp.int32)),
        in_specs=[IN_VMEM] * 2 + [ANYWHERE] + [IN_VMEM] * reach,
        out_specs=[IN_VMEM] * 2,
        scratch_shapes=[pltpu.VMEM(key.shape, bf16), pltpu.SemaphoreType.DMA(())],
        compiler_params=pltpu.CompilerParams(vmem_limit_bytes=VMEM_BYTES),
        cost_estimate=LONG,
        name="weigh",
    )(*in_vmem([flags, query]), *in_hbm([key_late]), *in_vmem([key, key_last, *with_pairs(key_near)]))

    value_near = after(token, value_near)
    swapped = [sent(x, pair) for x in value_near]
    value, value_last, *value_near = pull((value, value_last, *value_near))
    value_near = [x for both in zip(value_near, swapped) for x in both]
    return pl.pallas_call(
        functools.partial(sum_kernel, reach, group, kv_step),
        out_shape=jax.ShapeDtypeStruct((rows, query_width), bf16),
        in_specs=[IN_VMEM] * 2 + [ANYWHERE] + [IN_VMEM] * reach,
        out_specs=ANYWHERE,
        scratch_shapes=[
            pltpu.VMEM(value.shape, bf16),
            pltpu.VMEM((rows, query_width), bf16),
            pltpu.SemaphoreType.DMA(()),
            pltpu.SemaphoreType.DMA((kv_heads,)),
        ],
        compiler_params=pltpu.CompilerParams(vmem_limit_bytes=VMEM_BYTES),
        name="sum",
    )(*in_vmem([flags, weights]), *in_hbm([value_late]), *in_vmem([value, value_last, *value_near]))


def solution(mesh):
    placed = P(("dp", "blk", "head"), None)
    return jax.shard_map(
        functools.partial(on_device, mesh.shape["blk"]),
        mesh=mesh,
        in_specs=(placed, placed, placed, P("dp")),
        out_specs=placed,
        check_vma=False,
    )
```

```python
import functools
import math

import jax
import jax.numpy as jnp
import numpy as np
from jax import lax
from jax.experimental import pallas as pl
from jax.experimental.pallas import tpu as pltpu
from jax.sharding import PartitionSpec as P

HEAD_DIMENSION = 128
AXES = ("blk", "head")
EXP2_SCALE = math.log2(math.e) / math.sqrt(HEAD_DIMENSION)
VMEM_BYTES = 24 * 2**20
IN_VMEM = pl.BlockSpec(memory_space=pltpu.VMEM)
ANYWHERE = pl.BlockSpec(memory_space=pl.ANY)
LONG = pl.CostEstimate(flops=10**11, bytes_accessed=10**11, transcendentals=0)


def device_of(piece, blk_count):
    return 2 * piece if piece < blk_count else 2 * (2 * blk_count - 1 - piece) + 1


def as_devices(target_of, blk_count):
    return [(device_of(a, blk_count), device_of(b, blk_count)) for a, b in enumerate(target_of)]


def up_by(step, blk_count):
    pieces = 2 * blk_count
    return [p + step if p + step < pieces else pieces - 1 - p for p in range(pieces)]


def is_late(piece, distance, blk_count):
    turns = (piece < blk_count) & (piece + distance >= blk_count)
    return (piece % 2 == 1) & (piece + distance < 2 * blk_count) & ((piece % 4 == 3) | turns)


def early(distance, blk_count):
    target_of = []
    for p in range(2 * blk_count):
        first = p // blk_count * blk_count
        if p % 2 == 0:
            target_of.append(p + 1)
        elif p % 4 == 3:
            target_of.append(p - 1)
        else:
            target_of.append(first + (p - first + distance) % blk_count)
    return target_of


def late(distance, blk_count):
    above = up_by(distance, blk_count)
    return [p + 1 if p % 2 == 0 else above[p] for p in range(2 * blk_count)]


def my_piece(blk_count):
    index = lax.axis_index("blk")
    return jnp.where(lax.axis_index("head") == 0, index, 2 * blk_count - 1 - index)


def stage_kernel(blk_count, reach, docs_ref, code_ref, any_late_ref):
    distance = reach - 1
    any_late = jnp.int32(0)
    for p in range(2 * blk_count - distance):
        if is_late(p, distance, blk_count):
            any_late = any_late | (docs_ref[p] == docs_ref[p + distance]).astype(jnp.int32)
    any_late_ref[0] = any_late
    piece = my_piece(blk_count)
    doc = docs_ref[piece]
    count = jnp.int32(1)
    for back in range(1, reach):
        same = (piece >= back) & (docs_ref[jnp.maximum(piece - back, 0)] == doc)
        count = count + same.astype(jnp.int32)
    odd = piece % 2
    farthest = jnp.maximum(piece - distance, 0)
    comes_late = (count == reach) & (odd == 0) & is_late(farthest, distance, blk_count)
    code = count + 64 * odd + 128 * comes_late.astype(jnp.int32)
    code_ref[...] = jnp.full(code_ref.shape, code)


def blank_kernel(*refs):
    pass


def blank(arrays):
    return pl.pallas_call(
        blank_kernel,
        out_shape=tuple(jax.ShapeDtypeStruct(x.shape, x.dtype) for x in arrays),
        out_specs=(ANYWHERE,) * len(arrays),
        name="blank",
    )()


def pull_kernel(count, *refs):
    copies = [pltpu.make_async_copy(refs[i], refs[i - count - 1], refs[-1].at[i]) for i in range(count)]
    for copy in copies:
        copy.start()
    for copy in copies:
        copy.wait()


def pull(arrays, token=(), cost=None):
    return pl.pallas_call(
        functools.partial(pull_kernel, len(arrays)),
        out_shape=tuple(pltpu.VMEM(x.shape, x.dtype) for x in arrays),
        in_specs=[ANYWHERE] * len((*arrays, *token)),
        out_specs=[IN_VMEM] * len(arrays),
        scratch_shapes=[pltpu.SemaphoreType.DMA((len(arrays),))],
        compiler_params=pltpu.CompilerParams(vmem_limit_bytes=2**20),
        cost_estimate=cost,
        name="pull",
    )(*in_hbm([*arrays, *token]))


def read_code(code_ref):
    code = jnp.max(code_ref[...])
    return code % 64, code // 64 % 2 == 1, code // 128 == 1


def pick(odd, comes_late, last_ref, late_hbm, swapped, picked_ref, sem):
    @pl.when(odd)
    def _():
        for slot, ref in enumerate([last_ref, *swapped]):
            picked_ref[slot] = ref[...]

    @pl.when(jnp.logical_not(odd))
    def _():
        for slot, ref in enumerate(swapped):
            picked_ref[slot] = ref[...]

    @pl.when(jnp.logical_not(odd) & jnp.logical_not(comes_late))
    def _():
        picked_ref[len(swapped)] = last_ref[...]

    @pl.when(comes_late)
    def _():
        copy = pltpu.make_async_copy(late_hbm, picked_ref.at[len(swapped)], sem)
        copy.start()
        copy.wait()


def by_distance(own_ref, picked_ref, near):
    slots = [own_ref]
    for distance in range(1, 2 * picked_ref.shape[0]):
        slots.append(picked_ref.at[distance // 2] if distance % 2 else near[distance // 2 - 1])
    return slots


def by_count(count, reach, run):
    @pl.when(count >= reach - 1)
    def _():
        run(reach, reach - 1)

    @pl.when(count < reach - 1)
    def _():
        run(reach - 2, 1)


def lanes_at(index, width):
    return pl.ds(pl.multiple_of(index * width, width), width)


def weigh_kernel(reach, group, kv_step, code_ref, query_ref, late_hbm, own_ref, last_ref, *refs):
    near, swapped = refs[: reach // 2 - 1], refs[reach // 2 - 1 : -4]
    weight_ref, token_ref, picked_ref, sem = refs[-4:]
    token_ref[...] = code_ref[...]
    count, odd, comes_late = read_code(code_ref)
    pick(odd, comes_late, last_ref, late_hbm, swapped, picked_ref, sem)
    keys = by_distance(own_ref, picked_ref, near)
    rows = query_ref.shape[0]
    kv_heads = own_ref.shape[1] // HEAD_DIMENSION
    causal = lax.broadcasted_iota(jnp.int32, (rows, rows), 0) >= lax.broadcasted_iota(jnp.int32, (rows, rows), 1)

    def weigh(slots, first_masked):
        def one_step(step, _):
            for inner in range(kv_step):
                kv_head = step * kv_step + inner
                lanes = lanes_at(kv_head, HEAD_DIMENSION)
                key = jnp.concatenate([ref[:, lanes] for ref in keys[:slots]], axis=0)
                for member in range(group):
                    head = kv_head * group + member
                    query = query_ref[:, lanes_at(head, HEAD_DIMENSION)]
                    score = lax.dot_general(query, key, (((1,), (1,)), ((), ())), preferred_element_type=jnp.float32)
                    parts = [jnp.where(causal, score[:, :rows], -jnp.inf)]
                    for slot in range(1, slots):
                        part = score[:, slot * rows : (slot + 1) * rows]
                        parts.append(jnp.where(slot < count, part, -jnp.inf) if slot >= first_masked else part)
                    score = jnp.concatenate(parts, axis=1)
                    top = jnp.max(score, axis=1, keepdims=True)
                    weight = jnp.exp2((score - top) * EXP2_SCALE)
                    weight_ref[head, :, : slots * rows] = weight.astype(jnp.bfloat16)
            return 0

        lax.fori_loop(0, kv_heads // kv_step, one_step, 0)

    by_count(count, reach, weigh)


def sum_kernel(reach, group, kv_step, code_ref, weight_ref, late_hbm, own_ref, last_ref, *refs):
    near, swapped = refs[: reach // 2 - 1], refs[reach // 2 - 1 : -5]
    out_hbm, picked_ref, out_ref, sem, sems = refs[-5:]
    count, odd, comes_late = read_code(code_ref)
    pick(odd, comes_late, last_ref, late_hbm, swapped, picked_ref, sem)
    values = by_distance(own_ref, picked_ref, near)
    rows = out_ref.shape[0]
    kv_heads = own_ref.shape[1] // HEAD_DIMENSION
    width = group * HEAD_DIMENSION

    def send(kv_head):
        lanes = lanes_at(kv_head, width)
        return pltpu.make_async_copy(out_ref.at[:, lanes], out_hbm.at[:, lanes], sems.at[kv_head])

    def add_up(slots, first_masked):
        ones = jnp.ones((slots * rows, HEAD_DIMENSION), jnp.bfloat16)

        def one_step(step, _):
            for inner in range(kv_step):
                kv_head = step * kv_step + inner
                lanes = lanes_at(kv_head, HEAD_DIMENSION)
                value = jnp.concatenate([ref[:, lanes] for ref in values[:slots]], axis=0)
                value = jnp.concatenate([value, ones], axis=1)
                for member in range(group):
                    head = kv_head * group + member
                    weight = weight_ref[head, :, : slots * rows]
                    both = jnp.dot(weight, value, preferred_element_type=jnp.float32)
                    result = both[:, :HEAD_DIMENSION] / both[:, HEAD_DIMENSION:]
                    out_ref[:, lanes_at(head, HEAD_DIMENSION)] = result.astype(jnp.bfloat16)
                send(kv_head).start()
            return 0

        lax.fori_loop(0, kv_heads // kv_step, one_step, 0)

    by_count(count, reach, add_up)
    for kv_head in range(kv_heads):
        send(kv_head).wait()


def after_kernel(*refs):
    pass


def after(token, arrays, cost=None):
    return pl.pallas_call(
        after_kernel,
        out_shape=[jax.ShapeDtypeStruct(x.shape, x.dtype) for x in arrays],
        in_specs=[ANYWHERE] * (1 + len(arrays)),
        out_specs=[ANYWHERE] * len(arrays),
        input_output_aliases={1 + index: index for index in range(len(arrays))},
        compiler_params=pltpu.CompilerParams(vmem_limit_bytes=2**20),
        cost_estimate=cost,
        name="after",
    )(*in_vmem([token]), *arrays)


def in_vmem(arrays):
    return [pltpu.with_memory_space_constraint(x, pltpu.VMEM) for x in arrays]


def in_hbm(arrays):
    return [pltpu.with_memory_space_constraint(x, pltpu.HBM) for x in arrays]


def on_device(blk_count, query, key, value, docs):
    rows, query_width = query.shape
    kv_heads = key.shape[1] // HEAD_DIMENSION
    group = query_width // key.shape[1]
    heads = kv_heads * group
    reach = blk_count // 4
    distance = reach - 1
    kv_step = min(4, kv_heads)
    bf16 = jnp.bfloat16

    def sent(x, target_of):
        return lax.ppermute(x, AXES, as_devices(target_of, blk_count))

    pair = [p ^ 1 for p in range(2 * blk_count)]

    def near_of(x):
        return [sent(x, up_by(2 * step, blk_count)) for step in range(1, reach // 2)]

    key_near, key_last = near_of(key), sent(key, early(distance, blk_count))

    code, any_late = pl.pallas_call(
        functools.partial(stage_kernel, blk_count, reach),
        out_shape=(pltpu.VMEM((8, rows), jnp.int32), jax.ShapeDtypeStruct((1,), jnp.int32)),
        in_specs=[pl.BlockSpec(memory_space=pltpu.SMEM)],
        out_specs=[IN_VMEM, pl.BlockSpec(memory_space=pltpu.SMEM)],
        compiler_params=pltpu.CompilerParams(vmem_limit_bytes=2**20),
        name="stage",
    )(docs)
    any_late = any_late[0] > 0
    if lax.axis_size("dp") > 1:
        any_late = lax.pmax(any_late.astype(jnp.float32), "dp") > 0
    key_late, value_late = lax.cond(
        any_late,
        lambda: (sent(key, late(distance, blk_count)), sent(value, late(distance, blk_count))),
        lambda: blank((key, value)),
    )

    query, key, value = pull((query, key, value), (key_late,))
    value_near, value_last = near_of(value), sent(value, early(distance, blk_count))

    picked = pltpu.VMEM((reach // 2, *key.shape), bf16)
    key_near = after(value, key_near)
    (query,) = after(code, [query], LONG)
    key_swapped = [sent(x, pair) for x in key_near]
    weights, token = pl.pallas_call(
        functools.partial(weigh_kernel, reach, group, kv_step),
        out_shape=(pltpu.VMEM((heads, rows, reach * rows), bf16), pltpu.VMEM((8, rows), jnp.int32)),
        in_specs=[IN_VMEM] * 2 + [ANYWHERE] + [IN_VMEM] * reach,
        out_specs=[IN_VMEM] * 2,
        scratch_shapes=[picked, pltpu.SemaphoreType.DMA(())],
        compiler_params=pltpu.CompilerParams(vmem_limit_bytes=VMEM_BYTES),
        name="weigh",
    )(*in_vmem([code, query]), *in_hbm([key_late]), *in_vmem([key, key_last, *key_near, *key_swapped]))

    value_near = after(token, value_near)
    value_swapped = [sent(x, pair) for x in value_near]
    return pl.pallas_call(
        functools.partial(sum_kernel, reach, group, kv_step),
        out_shape=jax.ShapeDtypeStruct((rows, query_width), bf16),
        in_specs=[IN_VMEM] * 2 + [ANYWHERE] + [IN_VMEM] * reach,
        out_specs=ANYWHERE,
        scratch_shapes=[
            picked,
            pltpu.VMEM((rows, query_width), bf16),
            pltpu.SemaphoreType.DMA(()),
            pltpu.SemaphoreType.DMA((kv_heads,)),
        ],
        compiler_params=pltpu.CompilerParams(vmem_limit_bytes=VMEM_BYTES),
        name="sum",
    )(*in_vmem([code, weights]), *in_hbm([value_late]), *in_vmem([value, value_last, *value_near, *value_swapped]))


def solution(mesh):
    placed = P(("dp", "blk", "head"), None)
    return jax.shard_map(
        functools.partial(on_device, mesh.shape["blk"]),
        mesh=mesh,
        in_specs=(placed, placed, placed, P("dp")),
        out_specs=placed,
        check_vma=False,
    )
```

```python
import functools
import math

import jax
import jax.numpy as jnp
import numpy as np
from jax import lax
from jax.experimental import pallas as pl
from jax.experimental.pallas import tpu as pltpu
from jax.sharding import PartitionSpec as P

HEAD_DIMENSION = 128
AXES = ("blk", "head")
EXP2_SCALE = math.log2(math.e) / math.sqrt(HEAD_DIMENSION)
VMEM_BYTES = 24 * 2**20
IN_VMEM = pl.BlockSpec(memory_space=pltpu.VMEM)
ANYWHERE = pl.BlockSpec(memory_space=pl.ANY)
LONG = pl.CostEstimate(flops=10**11, bytes_accessed=10**11, transcendentals=0)


def device_of(piece, blk_count):
    return 2 * piece if piece < blk_count else 2 * (2 * blk_count - 1 - piece) + 1


def as_devices(target_of, blk_count):
    return [(device_of(a, blk_count), device_of(b, blk_count)) for a, b in enumerate(target_of)]


def up_by(step, blk_count):
    pieces = 2 * blk_count
    return [p + step if p + step < pieces else pieces - 1 - p for p in range(pieces)]


def is_late(piece, distance, blk_count):
    turns = (piece < blk_count) & (piece + distance >= blk_count)
    return (piece % 2 == 1) & (piece + distance < 2 * blk_count) & ((piece % 4 == 3) | turns)


def early(distance, blk_count):
    target_of = []
    for p in range(2 * blk_count):
        first = p // blk_count * blk_count
        if p % 2 == 0:
            target_of.append(p + 1)
        elif p % 4 == 3:
            target_of.append(p - 1)
        else:
            target_of.append(first + (p - first + distance) % blk_count)
    return target_of


def late(distance, blk_count):
    above = up_by(distance, blk_count)
    return [p + 1 if p % 2 == 0 else above[p] for p in range(2 * blk_count)]


def my_piece(blk_count):
    index = lax.axis_index("blk")
    return jnp.where(lax.axis_index("head") == 0, index, 2 * blk_count - 1 - index)


def stage_kernel(blk_count, reach, docs_ref, query_hbm, key_hbm, value_hbm, code_ref, any_late_ref, *refs):
    sources, sems = [query_hbm, key_hbm, value_hbm, value_hbm], refs[-1]
    copies = [pltpu.make_async_copy(x, refs[i], sems.at[i]) for i, x in enumerate(sources)]
    for copy in copies:
        copy.start()
    distance = reach - 1
    any_late = jnp.int32(0)
    for p in range(2 * blk_count - distance):
        if is_late(p, distance, blk_count):
            any_late = any_late | (docs_ref[p] == docs_ref[p + distance]).astype(jnp.int32)
    any_late_ref[0] = any_late
    piece = my_piece(blk_count)
    doc = docs_ref[piece]
    count = jnp.int32(1)
    for back in range(1, reach):
        same = (piece >= back) & (docs_ref[jnp.maximum(piece - back, 0)] == doc)
        count = count + same.astype(jnp.int32)
    odd = piece % 2
    farthest = jnp.maximum(piece - distance, 0)
    comes_late = (count == reach) & (odd == 0) & is_late(farthest, distance, blk_count)
    code = count + 64 * odd + 128 * comes_late.astype(jnp.int32)
    code_ref[...] = jnp.full(code_ref.shape, code)
    for copy in copies:
        copy.wait()


def blank_kernel(*refs):
    pass


def blank(arrays):
    return pl.pallas_call(
        blank_kernel,
        out_shape=tuple(jax.ShapeDtypeStruct(x.shape, x.dtype) for x in arrays),
        out_specs=(ANYWHERE,) * len(arrays),
        compiler_params=pltpu.CompilerParams(vmem_limit_bytes=2**20),
        name="blank",
    )()


def read_code(code_ref):
    code = jnp.max(code_ref[...])
    return code % 64, code // 64 % 2 == 1, code // 128 == 1


def pull_kernel(code_ref, *refs):
    count = len(refs) // 2
    _, _, comes_late = read_code(code_ref)

    @pl.when(comes_late)
    def _():
        copies = [pltpu.make_async_copy(refs[i], refs[count + i], refs[-1].at[i]) for i in range(count)]
        for copy in copies:
            copy.start()
        for copy in copies:
            copy.wait()


def pull(code, arrays):
    return pl.pallas_call(
        pull_kernel,
        out_shape=tuple(pltpu.VMEM(x.shape, x.dtype) for x in arrays),
        in_specs=[IN_VMEM] + [ANYWHERE] * len(arrays),
        out_specs=[IN_VMEM] * len(arrays),
        scratch_shapes=[pltpu.SemaphoreType.DMA((len(arrays),))],
        compiler_params=pltpu.CompilerParams(vmem_limit_bytes=2**20),
        name="pull",
    )(*in_vmem([code]), *in_hbm(arrays))


def pick(odd, comes_late, last_ref, late_ref, swapped, picked_ref):
    @pl.when(odd)
    def _():
        for slot, ref in enumerate([last_ref, *swapped]):
            picked_ref[slot] = ref[...]

    @pl.when(jnp.logical_not(odd))
    def _():
        for slot, ref in enumerate(swapped):
            picked_ref[slot] = ref[...]

    @pl.when(jnp.logical_not(odd) & jnp.logical_not(comes_late))
    def _():
        picked_ref[len(swapped)] = last_ref[...]

    @pl.when(comes_late)
    def _():
        picked_ref[len(swapped)] = late_ref[...]


def by_distance(own_ref, picked_ref, near):
    slots = [own_ref]
    for distance in range(1, 2 * picked_ref.shape[0]):
        slots.append(picked_ref.at[distance // 2] if distance % 2 else near[distance // 2 - 1])
    return slots


def by_count(count, reach, run):
    @pl.when(count >= reach - 1)
    def _():
        run(reach, reach - 1)

    @pl.when(count < reach - 1)
    def _():
        run(reach - 2, 1)


def lanes_at(index, width):
    return pl.ds(pl.multiple_of(index * width, width), width)


def weigh_kernel(reach, group, kv_step, code_ref, query_ref, late_ref, own_ref, last_ref, *refs):
    near, swapped = refs[: reach // 2 - 1], refs[reach // 2 - 1 : -3]
    weight_ref, token_ref, picked_ref = refs[-3:]
    token_ref[...] = code_ref[...]
    count, odd, comes_late = read_code(code_ref)
    pick(odd, comes_late, last_ref, late_ref, swapped, picked_ref)
    keys = by_distance(own_ref, picked_ref, near)
    rows = query_ref.shape[0]
    kv_heads = own_ref.shape[1] // HEAD_DIMENSION
    causal = lax.broadcasted_iota(jnp.int32, (rows, rows), 0) >= lax.broadcasted_iota(jnp.int32, (rows, rows), 1)

    def weigh(slots, first_masked):
        def one_step(step, _):
            for inner in range(kv_step):
                kv_head = step * kv_step + inner
                lanes = lanes_at(kv_head, HEAD_DIMENSION)
                key = jnp.concatenate([ref[:, lanes] for ref in keys[:slots]], axis=0)
                for member in range(group):
                    head = kv_head * group + member
                    query = query_ref[:, lanes_at(head, HEAD_DIMENSION)]
                    score = lax.dot_general(query, key, (((1,), (1,)), ((), ())), preferred_element_type=jnp.float32)
                    parts = [jnp.where(causal, score[:, :rows], -jnp.inf)]
                    for slot in range(1, slots):
                        part = score[:, slot * rows : (slot + 1) * rows]
                        parts.append(jnp.where(slot < count, part, -jnp.inf) if slot >= first_masked else part)
                    score = jnp.concatenate(parts, axis=1)
                    top = jnp.max(score, axis=1, keepdims=True)
                    weight = jnp.exp2((score - top) * EXP2_SCALE)
                    weight_ref[head, :, : slots * rows] = weight.astype(jnp.bfloat16)
            return 0

        lax.fori_loop(0, kv_heads // kv_step, one_step, 0)

    by_count(count, reach, weigh)


def sum_kernel(reach, group, kv_step, code_ref, weight_ref, late_ref, own_ref, last_ref, *refs):
    near, swapped = refs[: reach // 2 - 1], refs[reach // 2 - 1 : -4]
    out_hbm, picked_ref, out_ref, sems = refs[-4:]
    count, odd, comes_late = read_code(code_ref)
    pick(odd, comes_late, last_ref, late_ref, swapped, picked_ref)
    values = by_distance(own_ref, picked_ref, near)
    rows = out_ref.shape[0]
    kv_heads = own_ref.shape[1] // HEAD_DIMENSION
    width = group * HEAD_DIMENSION

    def send(kv_head):
        lanes = lanes_at(kv_head, width)
        return pltpu.make_async_copy(out_ref.at[:, lanes], out_hbm.at[:, lanes], sems.at[kv_head])

    def add_up(slots, first_masked):
        ones = jnp.ones((slots * rows, HEAD_DIMENSION), jnp.bfloat16)

        def one_step(step, _):
            for inner in range(kv_step):
                kv_head = step * kv_step + inner
                lanes = lanes_at(kv_head, HEAD_DIMENSION)
                value = jnp.concatenate([ref[:, lanes] for ref in values[:slots]], axis=0)
                value = jnp.concatenate([value, ones], axis=1)
                for member in range(group):
                    head = kv_head * group + member
                    weight = weight_ref[head, :, : slots * rows]
                    both = jnp.dot(weight, value, preferred_element_type=jnp.float32)
                    result = both[:, :HEAD_DIMENSION] / both[:, HEAD_DIMENSION:]
                    out_ref[:, lanes_at(head, HEAD_DIMENSION)] = result.astype(jnp.bfloat16)
                send(kv_head).start()
            return 0

        lax.fori_loop(0, kv_heads // kv_step, one_step, 0)

    by_count(count, reach, add_up)
    for kv_head in range(kv_heads):
        send(kv_head).wait()


def after_kernel(*refs):
    pass


def after(token, arrays, cost=None):
    return pl.pallas_call(
        after_kernel,
        out_shape=[jax.ShapeDtypeStruct(x.shape, x.dtype) for x in arrays],
        in_specs=[ANYWHERE] * (1 + len(arrays)),
        out_specs=[ANYWHERE] * len(arrays),
        input_output_aliases={1 + index: index for index in range(len(arrays))},
        compiler_params=pltpu.CompilerParams(vmem_limit_bytes=2**20),
        cost_estimate=cost,
        name="after",
    )(token, *arrays)


def in_vmem(arrays):
    return [pltpu.with_memory_space_constraint(x, pltpu.VMEM) for x in arrays]


def in_hbm(arrays):
    return [pltpu.with_memory_space_constraint(x, pltpu.HBM) for x in arrays]


def on_device(blk_count, query, key, value, docs):
    rows, query_width = query.shape
    kv_heads = key.shape[1] // HEAD_DIMENSION
    group = query_width // key.shape[1]
    heads = kv_heads * group
    reach = blk_count // 4
    distance = reach - 1
    kv_step = kv_heads
    bf16 = jnp.bfloat16

    def sent(x, target_of):
        return lax.ppermute(x, AXES, as_devices(target_of, blk_count))

    pair = [p ^ 1 for p in range(2 * blk_count)]

    def near_of(x):
        return [sent(x, up_by(2 * step, blk_count)) for step in range(1, reach // 2)]

    key_near, key_last = near_of(key), sent(key, early(distance, blk_count))

    code, any_late, query, own_key, own_value, sent_value = pl.pallas_call(
        functools.partial(stage_kernel, blk_count, reach),
        out_shape=(
            pltpu.VMEM((8, rows), jnp.int32),
            jax.ShapeDtypeStruct((1,), jnp.int32),
            *(pltpu.VMEM(x.shape, bf16) for x in (query, key, value, value)),
        ),
        in_specs=[pl.BlockSpec(memory_space=pltpu.SMEM)] + [ANYWHERE] * 3,
        out_specs=[IN_VMEM, pl.BlockSpec(memory_space=pltpu.SMEM)] + [IN_VMEM] * 4,
        scratch_shapes=[pltpu.SemaphoreType.DMA((4,))],
        compiler_params=pltpu.CompilerParams(vmem_limit_bytes=2**20),
        name="stage",
    )(docs, *in_hbm([query, key, value]))
    any_late = any_late[0] > 0
    if lax.axis_size("dp") > 1:
        any_late = lax.pmax(any_late.astype(jnp.float32), "dp") > 0
    key_late, value_late = lax.cond(
        any_late,
        lambda: (sent(key, late(distance, blk_count)), sent(value, late(distance, blk_count))),
        lambda: blank((key, value)),
    )

    own_value, sent_value = after(key_late, [own_value, sent_value])
    value_near, value_last = near_of(sent_value), sent(own_value, early(distance, blk_count))

    picked = pltpu.VMEM((reach // 2, *key.shape), bf16)
    key_near = after(own_key, key_near)
    (query,) = after(code, [query], LONG)
    key_late, value_late = pull(code, (key_late, value_late))
    key_swapped = [sent(x, pair) for x in key_near]
    weights, token = pl.pallas_call(
        functools.partial(weigh_kernel, reach, group, kv_step),
        out_shape=(pltpu.VMEM((heads, rows, reach * rows), bf16), pltpu.VMEM((8, rows), jnp.int32)),
        in_specs=[IN_VMEM] * (3 + reach),
        out_specs=[IN_VMEM] * 2,
        scratch_shapes=[picked],
        compiler_params=pltpu.CompilerParams(vmem_limit_bytes=VMEM_BYTES),
        name="weigh",
    )(*in_vmem([code, query, key_late, own_key, key_last, *key_near, *key_swapped]))

    value_near = after(token, value_near)
    value_swapped = [sent(x, pair) for x in value_near]
    return pl.pallas_call(
        functools.partial(sum_kernel, reach, group, kv_step),
        out_shape=jax.ShapeDtypeStruct((rows, query_width), bf16),
        in_specs=[IN_VMEM] * (3 + reach),
        out_specs=ANYWHERE,
        scratch_shapes=[
            picked,
            pltpu.VMEM((rows, query_width), bf16),
            pltpu.SemaphoreType.DMA((kv_heads,)),
        ],
        compiler_params=pltpu.CompilerParams(vmem_limit_bytes=VMEM_BYTES),
        name="sum",
    )(*in_vmem([code, weights, value_late, own_value, value_last, *value_near, *value_swapped]))


def solution(mesh):
    placed = P(("dp", "blk", "head"), None)
    return jax.shard_map(
        functools.partial(on_device, mesh.shape["blk"]),
        mesh=mesh,
        in_specs=(placed, placed, placed, P("dp")),
        out_specs=placed,
        check_vma=False,
    )
```

```python
import functools
import math

import jax
import jax.numpy as jnp
import numpy as np
from jax import lax
from jax.experimental import pallas as pl
from jax.experimental.pallas import tpu as pltpu
from jax.sharding import PartitionSpec as P

HEAD_DIMENSION = 128
AXES = ("blk", "head")
EXP2_SCALE = math.log2(math.e) / math.sqrt(HEAD_DIMENSION)
VMEM_BYTES = 24 * 2**20
IN_VMEM = pl.BlockSpec(memory_space=pltpu.VMEM)
ANYWHERE = pl.BlockSpec(memory_space=pl.ANY)
LONG = pl.CostEstimate(flops=10**11, bytes_accessed=10**11, transcendentals=0)


def device_of(piece, blk_count):
    return 2 * piece if piece < blk_count else 2 * (2 * blk_count - 1 - piece) + 1


def as_devices(target_of, blk_count):
    return [(device_of(a, blk_count), device_of(b, blk_count)) for a, b in enumerate(target_of)]


def up_by(step, blk_count):
    pieces = 2 * blk_count
    return [p + step if p + step < pieces else pieces - 1 - p for p in range(pieces)]


def is_late(piece, distance, blk_count):
    turns = (piece < blk_count) & (piece + distance >= blk_count)
    return (piece % 2 == 1) & (piece + distance < 2 * blk_count) & ((piece % 4 == 3) | turns)


def early(distance, blk_count):
    target_of = []
    for p in range(2 * blk_count):
        first = p // blk_count * blk_count
        if p % 2 == 0:
            target_of.append(p + 1)
        elif p % 4 == 3:
            target_of.append(p - 1)
        else:
            target_of.append(first + (p - first + distance) % blk_count)
    return target_of


def late(distance, blk_count):
    above = up_by(distance, blk_count)
    return [p + 1 if p % 2 == 0 else above[p] for p in range(2 * blk_count)]


def my_piece(blk_count):
    index = lax.axis_index("blk")
    return jnp.where(lax.axis_index("head") == 0, index, 2 * blk_count - 1 - index)


def stage_kernel(blk_count, reach, docs_hbm, query_hbm, key_hbm, value_hbm, code_ref, any_late_ref, *refs):
    sources, docs_ref, sems = [query_hbm, key_hbm, value_hbm, value_hbm], refs[-2], refs[-1]
    own_docs = pltpu.make_async_copy(docs_hbm, docs_ref, sems.at[len(sources)])
    own_docs.start()
    copies = [pltpu.make_async_copy(x, refs[i], sems.at[i]) for i, x in enumerate(sources)]
    for copy in copies:
        copy.start()
    own_docs.wait()
    distance = reach - 1
    any_late = jnp.int32(0)
    for p in range(2 * blk_count - distance):
        if is_late(p, distance, blk_count):
            any_late = any_late | (docs_ref[p] == docs_ref[p + distance]).astype(jnp.int32)
    any_late_ref[0] = any_late
    piece = my_piece(blk_count)
    doc = docs_ref[piece]
    count = jnp.int32(1)
    for back in range(1, reach):
        same = (piece >= back) & (docs_ref[jnp.maximum(piece - back, 0)] == doc)
        count = count + same.astype(jnp.int32)
    odd = piece % 2
    farthest = jnp.maximum(piece - distance, 0)
    comes_late = (count == reach) & (odd == 0) & is_late(farthest, distance, blk_count)
    code = count + 64 * odd + 128 * comes_late.astype(jnp.int32)
    code_ref[...] = jnp.full(code_ref.shape, code)
    for copy in copies:
        copy.wait()


def blank_kernel(*refs):
    pass


def blank(arrays):
    return pl.pallas_call(
        blank_kernel,
        out_shape=tuple(jax.ShapeDtypeStruct(x.shape, x.dtype) for x in arrays),
        out_specs=(ANYWHERE,) * len(arrays),
        compiler_params=pltpu.CompilerParams(vmem_limit_bytes=2**20),
        name="blank",
    )()


def read_code(code_ref):
    code = jnp.max(code_ref[...])
    return code % 64, code // 64 % 2 == 1, code // 128 == 1


def pull_kernel(code_ref, *refs):
    count = len(refs) // 2
    _, _, comes_late = read_code(code_ref)

    @pl.when(comes_late)
    def _():
        copies = [pltpu.make_async_copy(refs[i], refs[count + i], refs[-1].at[i]) for i in range(count)]
        for copy in copies:
            copy.start()
        for copy in copies:
            copy.wait()


def pull(code, arrays):
    return pl.pallas_call(
        pull_kernel,
        out_shape=tuple(pltpu.VMEM(x.shape, x.dtype) for x in arrays),
        in_specs=[IN_VMEM] + [ANYWHERE] * len(arrays),
        out_specs=[IN_VMEM] * len(arrays),
        scratch_shapes=[pltpu.SemaphoreType.DMA((len(arrays),))],
        compiler_params=pltpu.CompilerParams(vmem_limit_bytes=2**20),
        name="pull",
    )(*in_vmem([code]), *in_hbm(arrays))


def pick(odd, comes_late, last_ref, late_ref, swapped, picked_ref):
    @pl.when(odd)
    def _():
        for slot, ref in enumerate([last_ref, *swapped]):
            picked_ref[slot] = ref[...]

    @pl.when(jnp.logical_not(odd))
    def _():
        for slot, ref in enumerate(swapped):
            picked_ref[slot] = ref[...]

    @pl.when(jnp.logical_not(odd) & jnp.logical_not(comes_late))
    def _():
        picked_ref[len(swapped)] = last_ref[...]

    @pl.when(comes_late)
    def _():
        picked_ref[len(swapped)] = late_ref[...]


def by_distance(own_ref, picked_ref, near):
    slots = [own_ref]
    for distance in range(1, 2 * picked_ref.shape[0]):
        slots.append(picked_ref.at[distance // 2] if distance % 2 else near[distance // 2 - 1])
    return slots


def by_count(count, reach, run):
    @pl.when(count >= reach - 1)
    def _():
        run(reach, reach - 1)

    @pl.when(count < reach - 1)
    def _():
        run(reach - 2, 1)


def lanes_at(index, width):
    return pl.ds(pl.multiple_of(index * width, width), width)


def weigh_kernel(reach, group, kv_step, code_ref, query_ref, late_ref, own_ref, last_ref, *refs):
    near, swapped = refs[: reach // 2 - 1], refs[reach // 2 - 1 : -3]
    weight_ref, token_ref, picked_ref = refs[-3:]
    token_ref[...] = code_ref[...]
    count, odd, comes_late = read_code(code_ref)
    pick(odd, comes_late, last_ref, late_ref, swapped, picked_ref)
    keys = by_distance(own_ref, picked_ref, near)
    rows = query_ref.shape[0]
    kv_heads = own_ref.shape[1] // HEAD_DIMENSION
    causal = lax.broadcasted_iota(jnp.int32, (rows, rows), 0) >= lax.broadcasted_iota(jnp.int32, (rows, rows), 1)

    def weigh(slots, first_masked):
        def one_step(step, _):
            for inner in range(kv_step):
                kv_head = step * kv_step + inner
                lanes = lanes_at(kv_head, HEAD_DIMENSION)
                key = jnp.concatenate([ref[:, lanes] for ref in keys[:slots]], axis=0)
                for member in range(group):
                    head = kv_head * group + member
                    query = query_ref[:, lanes_at(head, HEAD_DIMENSION)]
                    score = lax.dot_general(query, key, (((1,), (1,)), ((), ())), preferred_element_type=jnp.float32)
                    parts = [jnp.where(causal, score[:, :rows], -jnp.inf)]
                    for slot in range(1, slots):
                        part = score[:, slot * rows : (slot + 1) * rows]
                        parts.append(jnp.where(slot < count, part, -jnp.inf) if slot >= first_masked else part)
                    score = jnp.concatenate(parts, axis=1)
                    top = jnp.max(score, axis=1, keepdims=True)
                    weight = jnp.exp2((score - top) * EXP2_SCALE)
                    weight_ref[head, :, : slots * rows] = weight.astype(jnp.bfloat16)
            return 0

        lax.fori_loop(0, kv_heads // kv_step, one_step, 0)

    by_count(count, reach, weigh)


def sum_kernel(reach, group, kv_step, code_ref, weight_ref, late_ref, own_ref, last_ref, *refs):
    near, swapped = refs[: reach // 2 - 1], refs[reach // 2 - 1 : -4]
    out_hbm, picked_ref, out_ref, sems = refs[-4:]
    count, odd, comes_late = read_code(code_ref)
    pick(odd, comes_late, last_ref, late_ref, swapped, picked_ref)
    values = by_distance(own_ref, picked_ref, near)
    rows = out_ref.shape[0]
    kv_heads = own_ref.shape[1] // HEAD_DIMENSION
    width = group * HEAD_DIMENSION

    def send(kv_head):
        lanes = lanes_at(kv_head, width)
        return pltpu.make_async_copy(out_ref.at[:, lanes], out_hbm.at[:, lanes], sems.at[kv_head])

    def add_up(slots, first_masked):
        ones = jnp.ones((slots * rows, HEAD_DIMENSION), jnp.bfloat16)

        def one_step(step, _):
            for inner in range(kv_step):
                kv_head = step * kv_step + inner
                lanes = lanes_at(kv_head, HEAD_DIMENSION)
                value = jnp.concatenate([ref[:, lanes] for ref in values[:slots]], axis=0)
                value = jnp.concatenate([value, ones], axis=1)
                for member in range(group):
                    head = kv_head * group + member
                    weight = weight_ref[head, :, : slots * rows]
                    both = jnp.dot(weight, value, preferred_element_type=jnp.float32)
                    result = both[:, :HEAD_DIMENSION] / both[:, HEAD_DIMENSION:]
                    out_ref[:, lanes_at(head, HEAD_DIMENSION)] = result.astype(jnp.bfloat16)
                send(kv_head).start()
            return 0

        lax.fori_loop(0, kv_heads // kv_step, one_step, 0)

    by_count(count, reach, add_up)
    for kv_head in range(kv_heads):
        send(kv_head).wait()


def after_kernel(*refs):
    pass


def after(token, arrays, cost=None):
    return pl.pallas_call(
        after_kernel,
        out_shape=[jax.ShapeDtypeStruct(x.shape, x.dtype) for x in arrays],
        in_specs=[ANYWHERE] * (1 + len(arrays)),
        out_specs=[ANYWHERE] * len(arrays),
        input_output_aliases={1 + index: index for index in range(len(arrays))},
        compiler_params=pltpu.CompilerParams(vmem_limit_bytes=2**20),
        cost_estimate=cost,
        name="after",
    )(token, *arrays)


def in_vmem(arrays):
    return [pltpu.with_memory_space_constraint(x, pltpu.VMEM) for x in arrays]


def in_hbm(arrays):
    return [pltpu.with_memory_space_constraint(x, pltpu.HBM) for x in arrays]


def on_device(blk_count, query, key, value, docs):
    rows, query_width = query.shape
    kv_heads = key.shape[1] // HEAD_DIMENSION
    group = query_width // key.shape[1]
    heads = kv_heads * group
    reach = blk_count // 4
    distance = reach - 1
    kv_step = kv_heads
    bf16 = jnp.bfloat16

    def sent(x, target_of):
        return lax.ppermute(x, AXES, as_devices(target_of, blk_count))

    pair = [p ^ 1 for p in range(2 * blk_count)]

    def near_of(x):
        return [sent(x, up_by(2 * step, blk_count)) for step in range(1, reach // 2)]

    key_near, key_last = near_of(key), sent(key, early(distance, blk_count))

    code, any_late, query, own_key, own_value, sent_value = pl.pallas_call(
        functools.partial(stage_kernel, blk_count, reach),
        out_shape=(
            pltpu.VMEM((8, rows), jnp.int32),
            jax.ShapeDtypeStruct((1,), jnp.int32),
            *(pltpu.VMEM(x.shape, bf16) for x in (query, key, value, value)),
        ),
        in_specs=[ANYWHERE] * 4,
        out_specs=[IN_VMEM, pl.BlockSpec(memory_space=pltpu.SMEM)] + [IN_VMEM] * 4,
        scratch_shapes=[pltpu.SMEM(docs.shape, jnp.int32), pltpu.SemaphoreType.DMA((5,))],
        compiler_params=pltpu.CompilerParams(vmem_limit_bytes=2**20),
        name="stage",
    )(*in_hbm([docs, query, key, value]))
    any_late = any_late[0] > 0
    if lax.axis_size("dp") > 1:
        any_late = lax.pmax(any_late.astype(jnp.float32), "dp") > 0
    key_late, value_late = lax.cond(
        any_late,
        lambda: (sent(key, late(distance, blk_count)), sent(value, late(distance, blk_count))),
        lambda: blank((key, value)),
    )

    own_value, sent_value = after(key_late, [own_value, sent_value])
    value_near, value_last = near_of(sent_value), sent(own_value, early(distance, blk_count))

    picked = pltpu.VMEM((reach // 2, *key.shape), bf16)
    key_near = after(own_key, key_near)
    (query,) = after(code, [query], LONG)
    key_late, value_late = pull(code, (key_late, value_late))
    key_swapped = [sent(x, pair) for x in key_near]
    weights, token = pl.pallas_call(
        functools.partial(weigh_kernel, reach, group, kv_step),
        out_shape=(pltpu.VMEM((heads, rows, reach * rows), bf16), pltpu.VMEM((8, rows), jnp.int32)),
        in_specs=[IN_VMEM] * (3 + reach),
        out_specs=[IN_VMEM] * 2,
        scratch_shapes=[picked],
        compiler_params=pltpu.CompilerParams(vmem_limit_bytes=VMEM_BYTES),
        name="weigh",
    )(*in_vmem([code, query, key_late, own_key, key_last, *key_near, *key_swapped]))

    value_near = after(token, value_near)
    value_swapped = [sent(x, pair) for x in value_near]
    return pl.pallas_call(
        functools.partial(sum_kernel, reach, group, kv_step),
        out_shape=jax.ShapeDtypeStruct((rows, query_width), bf16),
        in_specs=[IN_VMEM] * (3 + reach),
        out_specs=ANYWHERE,
        scratch_shapes=[
            picked,
            pltpu.VMEM((rows, query_width), bf16),
            pltpu.SemaphoreType.DMA((kv_heads,)),
        ],
        compiler_params=pltpu.CompilerParams(vmem_limit_bytes=VMEM_BYTES),
        name="sum",
    )(*in_vmem([code, weights, value_late, own_value, value_last, *value_near, *value_swapped]))


def solution(mesh):
    placed = P(("dp", "blk", "head"), None)
    return jax.shard_map(
        functools.partial(on_device, mesh.shape["blk"]),
        mesh=mesh,
        in_specs=(placed, placed, placed, P("dp")),
        out_specs=placed,
        check_vma=False,
    )
```
